512 devices in a mesh: dp: 16 (over z_hi, x, core), mp: 32 (over y, z_lo).
Axes of the slice: x: 4, y: 4, z: 16 (z_hi: 2, z_lo: 8; z = z_hi * 8 + z_lo), core: 2. Of those that a mesh axis runs over, the one named last changes fastest.
Arguments:
- accumulated: bfloat16 [16384, 28672], P('dp', 'mp'), may hold values from -6 to 6
- signs: int32 [8192], replicated, may hold values from 0 to 1
- q_start: bfloat16 [28672, 128], P('mp'), may hold values from -6 to 6
Outputs:
- new_error: bfloat16 [16384, 28672], P('dp', 'mp')
- p_basis: float32 [16384, 128], P('dp')
- q_factor: float32 [28672, 128], P('mp')
The draws below stay inside these ranges and needn't reach their ends.
Inputs may be any that keep to these rules, and one draw needn't show every extreme that they name: `signs`: 1 keeps a row's sign, 0 negates it.
All inputs are finite; a program needn't handle non-finite values.
Results may differ from the reference program's by a relative error of at most 0.0053.
Values may be sent and summed in bfloat16 or wider, within the bound.
A program may use at most 64 MiB of HBM per device.

```python
import math
import jax
import jax.numpy as jnp
from jax import lax

ROWS = 8192
FF = 28672
RANK = 128
REPLICAS = 2


def place_ends(values, key, smallest, high):
    longest = values.shape.index(max(values.shape))
    spots = []
    for shift in (0, 1):
        where = [jax.random.randint(jax.random.fold_in(key, axis), (), 0, length) for axis, length in enumerate(values.shape)]
        where[longest] = (where[longest] + shift) % values.shape[longest]
        spots.append(tuple(where))
    return values.at[spots[0]].set(smallest).at[spots[1]].set(high)


def steps_of(stream_key, shape, shards, least, high):
    factor_of = 1.0
    for axis_at, shards_of in shards:
        draws = jax.random.uniform(jax.random.fold_in(jax.random.fold_in(stream_key, 6), axis_at), (shards_of,), jnp.float32, least / len(shards), high / len(shards))
        factor_of = factor_of * jnp.repeat(jnp.exp(draws), shape[axis_at] // shards_of).reshape((-1,) + (1,) * (len(shape) - 1 - axis_at))
    return factor_of


def noise(stream_key, dims, deviation, reach, shards=(), kind=jnp.bfloat16):
    result = jax.random.normal(stream_key, dims, jnp.float32) * deviation
    if len(shards) > 0:
        result = steps_of(stream_key, dims, shards, -0.22, 0.18) * result
    return jnp.clip(result, min=-reach, max=reach).astype(kind)


def setup_inputs(seed: int = 0) -> dict:
    splits = jax.random.split(jax.random.key(seed), 4)
    accumulated = noise(splits[0], (REPLICAS * ROWS, FF), 1.0, 6.0, ((0, 16), (1, 32)))
    signs = place_ends(jax.random.randint(splits[1], (ROWS,), 0, 2), jax.random.fold_in(splits[1], 1), 0, 1).astype(jnp.int32)
    q_start = noise(splits[2], (FF, RANK), 1.0, 6.0, ((0, 32),))
    return dict(accumulated=accumulated, signs=signs, q_start=q_start)


def sylvester(size):
    index = jnp.arange(size, dtype=jnp.int32)
    both = index[:, None] & index[None, :]
    parity = jnp.zeros((size, size), jnp.int32)
    for shift in range(max(size.bit_length() - 1, 1)):
        parity = parity ^ both >> shift & 1
    return (1 - 2 * parity).astype(jnp.float32)

def rotate(block):
    total_rows, width = block.shape
    factors = []
    remaining = total_rows
    while remaining > 1:
        factor = min(32, remaining)
        factors.append(factor)
        remaining = remaining // factor
    if len(factors) == 0:
        return block
    cube = block.reshape(tuple(factors) + (width,))
    for which_axis, factor in enumerate(factors):
        cube = jnp.tensordot(sylvester(factor), cube, axes=([1], [which_axis]), precision=lax.Precision.HIGHEST)
        cube = jnp.moveaxis(cube, 0, which_axis)
    return cube.reshape(total_rows, width)

def reference(accumulated, signs, q_start):
    sign = (2 * signs - 1).astype(jnp.float32)
    blocks = accumulated.reshape(REPLICAS, ROWS, FF)

    def rotate_one(block):
        flipped = block.astype(jnp.float32) * sign[:, None]
        return (rotate(flipped) * (1.0 / math.sqrt(ROWS))).astype(jnp.bfloat16)
    rotated = lax.map(rotate_one, blocks)
    rotated = lax.optimization_barrier(rotated)

    def add_projection(total, block):
        return (total + jnp.dot(block.astype(jnp.float32), q_start.astype(jnp.float32), preferred_element_type=jnp.float32), None)
    projected, _ = lax.scan(add_projection, jnp.zeros((ROWS, RANK), jnp.float32), rotated)
    gram = jnp.dot(projected.T, projected, precision=lax.Precision.HIGHEST)
    lower = jnp.linalg.cholesky(gram)
    basis = jax.scipy.linalg.solve_triangular(lower, projected.T, lower=True).T
    basis16 = basis.astype(jnp.bfloat16)

    def add_right(total, block):
        return (total + jnp.dot(block.T.astype(jnp.float32), basis16.astype(jnp.float32), preferred_element_type=jnp.float32), None)
    q_total, _ = lax.scan(add_right, jnp.zeros((FF, RANK), jnp.float32), rotated)
    q_factor = q_total / REPLICAS
    q16 = q_factor.astype(jnp.bfloat16)
    approx = jnp.dot(basis16.astype(jnp.float32), q16.T.astype(jnp.float32), preferred_element_type=jnp.float32)

    def error_one(block):
        return (block.astype(jnp.float32) - approx).astype(jnp.bfloat16)
    new_error = lax.map(error_one, rotated).reshape(REPLICAS * ROWS, FF)
    p_basis = jnp.tile(basis, (REPLICAS, 1))
    return (new_error, p_basis, q_factor)
```

```python
import functools
import math

import jax
import jax.numpy as jnp
from jax import lax
from jax.experimental import pallas as pl
from jax.experimental.pallas import tpu as pltpu
from jax.sharding import PartitionSpec as P

MESH = pl.DeviceIdType.MESH
HIGH = lax.Precision.HIGHEST
REPLICAS, NX, NCORE, NY, ZLO = 2, 4, 2, 4, 8
NZ = REPLICAS * ZLO
NPOS = NX * NCORE
LANES = 128
SMALL = 256
F32, BF16 = jnp.float32, jnp.bfloat16


def parity_sign(rows, cols):
    i = lax.broadcasted_iota(jnp.int32, (rows, cols), 0)
    j = lax.broadcasted_iota(jnp.int32, (rows, cols), 1)
    both = i & j
    for shift in (4, 2, 1):
        both = both ^ (both >> shift)
    return (1 - 2 * (both & 1)).astype(F32)


def four(t):
    a, b, c, d = t[0] + t[1], t[0] - t[1], t[2] + t[3], t[2] - t[3]
    return (a + c, b + d, a - c, b - d)


def dot(a, b, **kw):
    return jnp.dot(a, b, preferred_element_type=F32, **kw)


def dot_t(a, b):
    return lax.dot_general(a, b, (((0,), (0,)), ((), ())), preferred_element_type=F32)


def kernel(a_ref, signs_ref, q_ref, err_ref, basis_ref, qf_ref,
           par, us, r1, wo, rot, hs, yp, ys, ybuf, zs, zbuf, vbuf, vz, yg, vg,
           gs, gcore, gsum, gx, ztp, ztc, zh, ztx, zx, ztz, zta, m_ref, n_ref,
           send, recv, rawsem, asem, bsem):
    dp, mp = lax.axis_index("dp"), lax.axis_index("mp")
    zhi, pos = dp // NPOS, dp % NPOS
    x, core = pos // NCORE, pos % NCORE
    y, zlo = mp // ZLO, mp % ZLO
    z = zhi * ZLO + zlo
    rows, cols = a_ref.shape
    groups = cols // LANES
    quarter = rows // NX
    yrows = rows // NY
    zrows = yrows // NZ
    rank = q_ref.shape[1]
    scale = 1.0 / math.sqrt(rows * NPOS)

    def at_y(k):
        yy = (y + k) % NY
        return yy, (dp, yy * ZLO + zlo)

    def at_z(k):
        zz = (z + k) % NZ
        return zz, ((zz // ZLO) * NPOS + pos, y * ZLO + zz % ZLO)

    def at_pos(k):
        pp = (pos + k) % NPOS
        return (zhi * NPOS + pp, mp)

    def at_x(k):
        xx = (x + k) % NX
        return xx, (zhi * NPOS + xx * NCORE + core, mp)

    other_core = (zhi * NPOS + x * NCORE + 1 - core, mp)
    other_rep = ((1 - zhi) * NPOS + pos, mp)

    def start(src, dst, s, r, device):
        pltpu.make_async_remote_copy(
            src_ref=src, dst_ref=dst, send_sem=s, recv_sem=r, device_id=device, device_id_type=MESH
        ).start()

    def wait(ref, sem):
        pltpu.make_async_copy(ref, ref, sem).wait()

    sent = []

    def lanes(g):
        return pl.ds(g * LANES, LANES)

    barrier = pltpu.get_barrier_semaphore()
    partners = [at_y(k)[1] for k in range(1, NY)] + [at_z(k)[1] for k in range(1, NZ)]
    partners += [at_pos(k) for k in range(1, NPOS)]
    for device in partners:
        pl.semaphore_signal(barrier, inc=1, device_id=device, device_id_type=MESH)

    yp[...] = dot(a_ref[...], q_ref[...])
    ys[...] = yp[...].astype(BF16)
    small = parity_sign(SMALL, SMALL)
    mine = (2 * signs_ref[pl.ds(pl.multiple_of(pos * 8, 8), 8), :] - 1).astype(F32)
    theirs_at = pos + 1 - 2 * core
    theirs = (2 * signs_ref[pl.ds(pl.multiple_of(theirs_at * 8, 8), 8), :] - 1).astype(F32)
    core_sign = (1 - 2 * core).astype(F32)
    for a in range(NX):
        row = jnp.concatenate([mine[2 * a : 2 * a + 1], mine[2 * a + 1 : 2 * a + 2]], axis=1)
        hs[a] = (small * (row * core_sign)).astype(BF16)
        row = jnp.concatenate([theirs[2 * a : 2 * a + 1], theirs[2 * a + 1 : 2 * a + 2]], axis=1)
        hs[NX + a] = (small * row).astype(BF16)

    pl.semaphore_wait(barrier, len(partners))

    for g in range(groups):
        start(a_ref.at[:, lanes(g)], par.at[:, lanes(g)], send.at[0], rawsem.at[g], other_core)
    sent.append((a_ref, 0))

    for k in range(1, NY):
        yy, device = at_y(k)
        start(ys.at[pl.ds(pl.multiple_of(yy * yrows, yrows), yrows), :], ybuf.at[k - 1],
              send.at[1], recv.at[1], device)
    sent.append((ybuf, 1))

    def transform(g):
        wait(par.at[:, lanes(g)], rawsem.at[g])
        t = []
        for a in range(NX):
            part = pl.ds(a * SMALL, SMALL)
            t.append(dot(hs[a], a_ref[part, lanes(g)]) + dot(hs[NX + a], par[part, lanes(g)]))
        for s, u in enumerate(four(t)):
            us[s, :, lanes(g)] = u.astype(BF16)
        r1[x, :, lanes(g)] = us[x, :, lanes(g)]
        for k in range(1, NX):
            xx, device = at_x(k)
            start(us.at[xx, :, lanes(g)], r1.at[x, :, lanes(g)], send.at[2], asem.at[g], device)

    def mix(g):
        wait(r1.at[0 : NX - 1, :, lanes(g)], asem.at[g])
        u = [r1[s, :, lanes(g)].astype(F32) for s in range(NX)]
        for s, w in enumerate(four(u)):
            wo[s, :, lanes(g)] = (w * scale).astype(BF16)
        rot[x, :, lanes(g)] = wo[x, :, lanes(g)]
        for k in range(1, NX):
            xx, device = at_x(k)
            start(wo.at[xx, :, lanes(g)], rot.at[x, :, lanes(g)], send.at[3], bsem.at[g], device)

    for g in range(3):
        transform(g)

    wait(ybuf, recv.at[1])
    total = yp[pl.ds(pl.multiple_of(y * yrows, yrows), yrows), :]
    for k in range(NY - 1):
        total = total + ybuf[k].astype(F32)
    zs[...] = total.astype(BF16)
    yp[0:yrows, :] = total
    for k in range(1, NZ):
        zz, device = at_z(k)
        start(zs.at[pl.ds(pl.multiple_of(zz * zrows, zrows), zrows), :], zbuf.at[k - 1],
              send.at[4], recv.at[4], device)
    sent.append((zbuf, 4))

    for g in range(3, groups):
        transform(g)
    for s in (2, 3):
        sent.append((r1.at[0 : NX - 1], s))

    wait(zbuf, recv.at[4])
    total = yp[pl.ds(pl.multiple_of(z * zrows, zrows), zrows), :]
    for k in range(NZ - 1):
        total = total + zbuf[k].astype(F32)
    own_rows = pl.multiple_of(y * yrows + z * zrows, zrows)
    yg[pl.ds(own_rows, zrows), :] = total.astype(BF16)
    for k in range(1, NZ):
        _, device = at_z(k)
        own = yg.at[pl.ds(own_rows, zrows), :]
        start(own, own, send.at[5], recv.at[5], device)
    sent.append((zbuf, 5))

    line = (2 * signs_ref[pl.ds(pos * 8 + own_rows // LANES, 1), :] - 1).astype(F32)
    spot = lax.broadcasted_iota(jnp.int32, (zrows, LANES), 0) + own_rows % LANES
    lane = lax.broadcasted_iota(jnp.int32, (zrows, LANES), 1)
    sign = jnp.sum(jnp.where(lane == spot, line, 0.0), axis=1, keepdims=True)
    vbuf[pos] = total * sign
    for k in range(1, NPOS):
        start(vbuf.at[pos], vbuf.at[pos], send.at[6], recv.at[6], at_pos(k))
    sent.append((vbuf.at[0 : NPOS - 1], 6))

    wait(zbuf, recv.at[5])
    for k in range(1, NY):
        _, device = at_y(k)
        own = yg.at[pl.ds(pl.multiple_of(y * yrows, yrows), yrows), :]
        start(own, own, send.at[7], recv.at[7], device)
    sent.append((ybuf, 7))

    wait(vbuf.at[0 : NPOS - 1], recv.at[6])
    mixed = jnp.zeros((zrows, rank), F32)
    for s in range(NPOS):
        bits = (pos % 2) * (s % 2) + (pos // 2 % 2) * (s // 2 % 2) + (pos // 4) * (s // 4)
        mixed = mixed + vbuf[s] * (1 - 2 * (bits % 2)).astype(F32)
    vg[pl.ds(own_rows, zrows), :] = mixed.astype(BF16)
    for k in range(1, NZ):
        _, device = at_z(k)
        own = vg.at[pl.ds(own_rows, zrows), :]
        start(own, own, send.at[8], recv.at[8], device)
    sent.append((zbuf, 8))

    wait(ybuf, recv.at[7])
    gs[...] = dot_t(yg[...], yg[...])
    start(gs, gcore, send.at[9], recv.at[9], other_core)
    sent.append((gs, 9))
    ztp[...] = dot_t(yg[...], a_ref[...])
    half = rank // NCORE
    theirs_half = pl.ds(pl.multiple_of((1 - core) * half, half), half)
    start(ztp.at[theirs_half, :], ztc, send.at[10], recv.at[10], other_core)
    sent.append((ztc, 10))

    wait(zbuf, recv.at[8])
    for k in range(1, NY):
        _, device = at_y(k)
        own = vg.at[pl.ds(pl.multiple_of(y * yrows, yrows), yrows), :]
        start(own, own, send.at[11], recv.at[11], device)
    sent.append((ybuf, 11))

    wait(gcore, recv.at[9])
    gx[x] = gs[...] + gcore[...]
    for k in range(1, NX):
        _, device = at_x(k)
        start(gx.at[x], gx.at[x], send.at[12], recv.at[12], device)
    sent.append((gx.at[0 : NX - 1], 12))

    wait(ztc, recv.at[10])
    part = rank // NPOS
    zh[...] = ztp[pl.ds(pl.multiple_of(core * half, half), half), :] + ztc[...]
    for k in range(1, NX):
        xx, device = at_x(k)
        start(zh.at[pl.ds(pl.multiple_of(xx * part, part), part), :], ztx.at[k - 1],
              send.at[13], recv.at[13], device)
    sent.append((ztx, 13))

    for g in range(groups):
        mix(g)

    wait(ztx, recv.at[13])
    total = zh[pl.ds(pl.multiple_of(x * part, part), part), :]
    for k in range(NX - 1):
        total = total + ztx[k]
    zx[...] = total
    start(zx, ztz, send.at[14], recv.at[14], other_rep)
    sent.append((zx, 14))

    wait(gx.at[0 : NX - 1], recv.at[12])
    m_ref[...] = gx[0] + gx[1] + gx[2] + gx[3]
    ri = lax.broadcasted_iota(jnp.int32, (rank, rank), 0)
    ci = lax.broadcasted_iota(jnp.int32, (rank, rank), 1)
    n_ref[...] = jnp.where(ri == ci, 1.0, 0.0).astype(F32)

    def eliminate(j, carry):
        m = m_ref[...]
        row = m_ref[pl.ds(j, 1), :]
        nrow = n_ref[pl.ds(j, 1), :]
        pivot = jnp.sum(jnp.where(ci[0:1] == j, row, 0.0), axis=1, keepdims=True)
        col = jnp.sum(jnp.where(ci == j, m, 0.0), axis=1, keepdims=True)
        col = jnp.where(ri[:, 0:1] > j, col / pivot, 0.0)
        m_ref[...] = m - col * row
        n_ref[...] = n_ref[...] - col * nrow
        return carry

    lax.fori_loop(0, rank, eliminate, 0)
    pivots = jnp.sum(jnp.where(ri == ci, m_ref[...], 0.0), axis=1, keepdims=True)
    inverse = n_ref[...] * (1.0 / jnp.sqrt(pivots))

    wait(ztz, recv.at[14])
    rank_rows = pl.multiple_of(core * half + x * part, part)
    zta[pl.ds(rank_rows, part), :] = zx[...] + ztz[...]
    for k in range(1, NX):
        _, device = at_x(k)
        own = zta.at[pl.ds(rank_rows, part), :]
        start(own, own, send.at[15], recv.at[15], device)
    sent.append((ztx, 15))

    wait(ybuf, recv.at[11])
    t = []
    small16 = small.astype(BF16)
    for a in range(NX):
        t.append(dot(small16, vg[a * SMALL : (a + 1) * SMALL, :]))
    for a, v in enumerate(four(t)):
        basis_ref[a * SMALL : (a + 1) * SMALL, :] = lax.dot_general(
            v * scale, inverse, (((1,), (1,)), ((), ())), precision=HIGH, preferred_element_type=F32
        )

    wait(ztx, recv.at[15])
    own = zta.at[pl.ds(pl.multiple_of(core * half, half), half), :]
    start(own, own, send.at[16], recv.at[16], other_core)
    sent.append((ztc, 16))
    wait(ztc, recv.at[16])
    right = dot(inverse, zta[...], precision=HIGH) * (1.0 / REPLICAS)
    for g in range(groups):
        qf_ref[lanes(g), :] = right[:, g * LANES : (g + 1) * LANES].T
    right16 = right.astype(BF16)

    for g in range(groups):
        wait(rot.at[0 : NX - 1, :, lanes(g)], bsem.at[g])
    for a in range(NX):
        part_rows = pl.ds(a * SMALL, SMALL)
        approx = dot(basis_ref[part_rows, :].astype(BF16), right16)
        err_ref[part_rows, :] = (rot[a].astype(F32) - approx).astype(BF16)
    for ref, s in sent:
        wait(ref, send.at[s])


def local(accumulated, signs, q_start):
    rows, cols = accumulated.shape
    rank = q_start.shape[1]
    quarter, yrows = rows // NX, rows // NY
    zrows, half, part = yrows // NZ, rank // NCORE, rank // NPOS
    groups = cols // LANES
    vmem = pl.BlockSpec(memory_space=pltpu.VMEM)
    dma = pltpu.SemaphoreType.DMA
    scratch = [
        ((rows, cols), BF16), ((NX, quarter, cols), BF16), ((NX, quarter, cols), BF16),
        ((NX, quarter, cols), BF16), ((NX, quarter, cols), BF16), ((2 * NX, SMALL, SMALL), BF16),
        ((rows, rank), F32), ((rows, rank), BF16), ((NY - 1, yrows, rank), BF16),
        ((yrows, rank), BF16), ((NZ - 1, zrows, rank), BF16), ((NPOS, zrows, rank), F32),
        ((zrows, rank), BF16), ((rows, rank), BF16), ((rows, rank), BF16),
        ((rank, rank), F32), ((rank, rank), F32), ((rank, rank), F32), ((NX, rank, rank), F32),
        ((rank, cols), F32), ((half, cols), F32), ((half, cols), F32), ((NX - 1, part, cols), F32),
        ((part, cols), F32), ((part, cols), F32), ((rank, cols), F32),
        ((rank, rank), F32), ((rank, rank), F32),
    ]
    return pl.pallas_call(
        kernel,
        out_shape=(
            jax.ShapeDtypeStruct((rows, cols), BF16),
            jax.ShapeDtypeStruct((rows, rank), F32),
            jax.ShapeDtypeStruct((cols, rank), F32),
        ),
        in_specs=[vmem] * 3,
        out_specs=(vmem,) * 3,
        scratch_shapes=[pltpu.VMEM(shape, kind) for shape, kind in scratch]
        + [dma((17,)), dma((17,)), dma((groups,)), dma((groups,)), dma((groups,))],
        compiler_params=pltpu.CompilerParams(
            collective_id=0, has_side_effects=True, vmem_limit_bytes=48 * 1024 * 1024
        ),
        name="powersgd",
    )(accumulated, signs.reshape(-1, LANES), q_start)


def solution(mesh):
    in_specs = (P("dp", "mp"), P(), P("mp", None))
    out_specs = (P("dp", "mp"), P("dp", None), P("mp", None))
    return jax.shard_map(local, mesh=mesh, in_specs=in_specs, out_specs=out_specs, check_vma=False)
```

```python
import functools
import math

import jax
import jax.numpy as jnp
from jax import lax
from jax.experimental import pallas as pl
from jax.experimental.pallas import tpu as pltpu
from jax.sharding import PartitionSpec as P

MESH = pl.DeviceIdType.MESH
HIGH = lax.Precision.HIGHEST
REPLICAS, NX, NCORE, NY, ZLO = 2, 4, 2, 4, 8
NZ = REPLICAS * ZLO
NPOS = NX * NCORE
LANES = 128
FAR_FIRST = (8, 7, 9, 6, 10, 5, 11, 4, 12, 3, 13, 2, 14, 1, 15)
SMALL = 256
F32, BF16 = jnp.float32, jnp.bfloat16


def parity_sign(rows, cols):
    i = lax.broadcasted_iota(jnp.int32, (rows, cols), 0)
    j = lax.broadcasted_iota(jnp.int32, (rows, cols), 1)
    both = i & j
    for shift in (4, 2, 1):
        both = both ^ (both >> shift)
    return (1 - 2 * (both & 1)).astype(F32)


def four(t):
    a, b, c, d = t[0] + t[1], t[0] - t[1], t[2] + t[3], t[2] - t[3]
    return (a + c, b + d, a - c, b - d)


def dot(a, b, **kw):
    return jnp.dot(a, b, preferred_element_type=F32, **kw)


def dot_t(a, b):
    return lax.dot_general(a, b, (((0,), (0,)), ((), ())), preferred_element_type=F32)


def wide(v, width):
    return jnp.broadcast_to(v, (1, width))


def inverse_cholesky(m, out_ref, step):
    rank = m.shape[0]
    ri = lax.broadcasted_iota(jnp.int32, (rank, rank), 0)
    ci = lax.broadcasted_iota(jnp.int32, (rank, rank), 1)
    n = jnp.where(ri == ci, 1.0, 0.0).astype(F32)
    for j in range(0, rank, step):
        span = range(step)
        r = [m[j + a : j + a + 1, :] for a in span]
        s = [n[j + a : j + a + 1, :] for a in span]
        p = [[wide(r[a][:, j + b : j + b + 1], rank) if b >= a else None for b in span] for a in span]
        low = [[None] * step for _ in span]
        inv = [None] * step
        for a in span:
            inv[a] = 1.0 / p[a][a]
            for b in range(a + 1, step):
                low[b][a] = p[a][b] * inv[a]
                for c in range(b, step):
                    p[b][c] = p[b][c] - low[b][a] * p[a][c]
                r[b] = r[b] - low[b][a] * r[a]
                s[b] = s[b] - low[b][a] * s[a]
        w, v = [None] * step, [None] * step
        for a in reversed(span):
            w[a], v[a] = r[a] * inv[a], s[a] * inv[a]
            for b in range(a + 1, step):
                w[a] = w[a] - low[b][a] * w[b]
                v[a] = v[a] - low[b][a] * v[b]
        for a in span:
            out_ref[j + a : j + a + 1, :] = s[a] * (1.0 / jnp.sqrt(p[a][a]))
        if j + step < rank:
            cols = [jnp.broadcast_to(m[:, j + a : j + a + 1], m.shape) for a in span]
            for a in span:
                m = m - cols[a] * w[a]
                n = n - cols[a] * v[a]


def kernel(a_hbm, signs_hbm, q_hbm, err_ref, basis_ref, qf_ref,
           a_ref, signs_ref, q_ref,
           par, us, r1, wo, rot, hs, yp, ys, ybuf, zs, zbuf, vbuf, yg, vg,
           gs, gcore, gx, gall, ztp, ztc, zh, ztx, zx, ztz, zta, inv_ref,
           send, recv, rawsem, asem, bsem, insem):
    dp, mp = lax.axis_index("dp"), lax.axis_index("mp")
    zhi, pos = dp // NPOS, dp % NPOS
    x, core = pos // NCORE, pos % NCORE
    y, zlo = mp // ZLO, mp % ZLO
    z = zhi * ZLO + zlo
    rows, cols = a_ref.shape
    groups = cols // LANES
    yrows = rows // NY
    zrows = yrows // NZ
    rank = q_ref.shape[1]
    scale = 1.0 / math.sqrt(rows * NPOS)

    def at_y(k):
        yy = (y + k) % NY
        return yy, (dp, yy * ZLO + zlo)

    def at_z(k):
        zz = (z + k) % NZ
        return zz, ((zz // ZLO) * NPOS + pos, y * ZLO + zz % ZLO)

    def at_pos(k):
        return (zhi * NPOS + (pos + k) % NPOS, mp)

    def at_x(k):
        xx = (x + k) % NX
        return xx, (zhi * NPOS + xx * NCORE + core, mp)

    other_core = (zhi * NPOS + x * NCORE + 1 - core, mp)
    other_rep = ((1 - zhi) * NPOS + pos, mp)

    def start(src, dst, s, r, device):
        pltpu.make_async_remote_copy(
            src_ref=src, dst_ref=dst, send_sem=s, recv_sem=r, device_id=device, device_id_type=MESH
        ).start()

    def wait(ref, sem):
        pltpu.make_async_copy(ref, ref, sem).wait()

    def lanes(g):
        return pl.ds(g * LANES, LANES)

    def some(first, count):
        return pl.ds(pl.multiple_of(first, count), count)

    sent = []

    barrier = pltpu.get_barrier_semaphore()
    partners = [at_z(k)[1] for k in FAR_FIRST] + [at_y(k)[1] for k in range(1, NY)]
    partners += [at_pos(k) for k in range(1, NPOS)]
    for device in partners:
        pl.semaphore_signal(barrier, inc=1, device_id=device, device_id_type=MESH)

    loads = [pltpu.make_async_copy(src, dst, insem.at[i])
             for i, (src, dst) in enumerate(((signs_hbm, signs_ref), (q_hbm, q_ref), (a_hbm, a_ref)))]
    for load in loads:
        load.start()
    loads[0].wait()
    small = parity_sign(SMALL, SMALL)
    mine = (2 * signs_ref[some(pos * 8, 8), :] - 1).astype(F32)
    theirs = (2 * signs_ref[some((pos + 1 - 2 * core) * 8, 8), :] - 1).astype(F32)
    core_sign = (1 - 2 * core).astype(F32)
    for a in range(NX):
        row = jnp.concatenate([mine[2 * a : 2 * a + 1], mine[2 * a + 1 : 2 * a + 2]], axis=1)
        hs[a] = (small * (row * core_sign)).astype(BF16)
        row = jnp.concatenate([theirs[2 * a : 2 * a + 1], theirs[2 * a + 1 : 2 * a + 2]], axis=1)
        hs[NX + a] = (small * row).astype(BF16)
    loads[1].wait()
    loads[2].wait()
    yp[...] = dot(a_ref[...], q_ref[...])
    ys[...] = yp[...].astype(BF16)

    pl.semaphore_wait(barrier, len(partners))

    for k in (2, 1, 3):
        yy, device = at_y(k)
        start(ys.at[some(yy * yrows, yrows), :], ybuf.at[k - 1], send.at[1], recv.at[1], device)
    sent.append((ybuf, 1))

    for g in range(groups):
        start(a_ref.at[:, lanes(g)], par.at[g], send.at[0], rawsem.at[g], other_core)
    sent.append((par, 0))

    def transform(g):
        wait(par.at[g], rawsem.at[g])
        t = []
        for a in range(NX):
            part = pl.ds(a * SMALL, SMALL)
            t.append(dot(hs[a], a_ref[part, lanes(g)]) + dot(hs[NX + a], par[g, part, :]))
        for s, u in enumerate(four(t)):
            us[g, s] = u.astype(BF16)
        r1[g, x] = us[g, x]
        for k in range(1, NX):
            xx, device = at_x(k)
            start(us.at[g, xx], r1.at[g, x], send.at[2], asem.at[g], device)

    def mix(g):
        wait(r1.at[g, 0 : NX - 1], asem.at[g])
        u = [r1[g, s].astype(F32) for s in range(NX)]
        for s, w in enumerate(four(u)):
            wo[g, s] = (w * scale).astype(BF16)
        rot[g, x] = wo[g, x]
        for k in range(1, NX):
            xx, device = at_x(k)
            start(wo.at[g, xx], rot.at[g, x], send.at[3], bsem.at[g], device)

    for g in range(groups):
        transform(g)
    for s in (2, 3):
        sent.append((r1.at[:, 0 : NX - 1], s))

    wait(ybuf, recv.at[1])
    total = yp[some(y * yrows, yrows), :]
    for k in range(NY - 1):
        total = total + ybuf[k].astype(F32)
    zs[...] = total.astype(BF16)
    yp[0:yrows, :] = total
    for k in FAR_FIRST:
        zz, device = at_z(k)
        start(zs.at[some(zz * zrows, zrows), :], zbuf.at[k - 1], send.at[4], recv.at[4], device)
    sent.append((zbuf, 4))

    wait(zbuf, recv.at[4])
    total = yp[some(z * zrows, zrows), :]
    for k in range(NZ - 1):
        total = total + zbuf[k].astype(F32)
    own_rows = pl.multiple_of(y * yrows + z * zrows, zrows)
    own = yg.at[pl.ds(own_rows, zrows), :]
    own[...] = total.astype(BF16)
    for k in FAR_FIRST:
        start(own, own, send.at[5], recv.at[5], at_z(k)[1])
    sent.append((zbuf, 5))

    line = (2 * signs_ref[pl.ds(pos * 8 + own_rows // LANES, 1), :] - 1).astype(F32)
    spot = lax.broadcasted_iota(jnp.int32, (zrows, LANES), 0) + own_rows % LANES
    lane = lax.broadcasted_iota(jnp.int32, (zrows, LANES), 1)
    sign = jnp.sum(jnp.where(lane == spot, line, 0.0), axis=1, keepdims=True)
    vbuf[pos] = total * sign
    for k in range(1, NPOS):
        start(vbuf.at[pos], vbuf.at[pos], send.at[6], recv.at[6], at_pos(k))
    sent.append((vbuf.at[0 : NPOS - 1], 6))

    mix(0)
    wait(zbuf, recv.at[5])
    block = yg.at[some(y * yrows, yrows), :]
    for k in (2, 1, 3):
        start(block, block, send.at[7], recv.at[7], at_y(k)[1])
    sent.append((ybuf, 7))

    wait(vbuf.at[0 : NPOS - 1], recv.at[6])
    mixed = jnp.zeros((zrows, rank), F32)
    for s in range(NPOS):
        bits = (pos % 2) * (s % 2) + (pos // 2 % 2) * (s // 2 % 2) + (pos // 4) * (s // 4)
        mixed = mixed + vbuf[s] * (1 - 2 * (bits % 2)).astype(F32)
    own_v = vg.at[pl.ds(own_rows, zrows), :]
    own_v[...] = mixed.astype(BF16)
    for k in FAR_FIRST:
        start(own_v, own_v, send.at[8], recv.at[8], at_z(k)[1])
    sent.append((zbuf, 8))
    mix(1)

    wait(ybuf, recv.at[7])
    half, part = rank // NCORE, rank // NPOS
    ztp[...] = dot_t(yg[...], a_ref[...])
    start(ztp.at[some((1 - core) * half, half), :], ztc, send.at[10], recv.at[10], other_core)
    sent.append((ztc, 10))
    gs[...] = dot_t(yg[...], yg[...])
    start(gs, gcore, send.at[9], recv.at[9], other_core)
    sent.append((gs, 9))

    wait(ztc, recv.at[10])
    zh[...] = ztp[some(core * half, half), :] + ztc[...]
    for k in (2, 1, 3):
        xx, device = at_x(k)
        start(zh.at[some(xx * part, part), :], ztx.at[k - 1], send.at[13], recv.at[13], device)
    sent.append((ztx, 13))

    wait(gcore, recv.at[9])
    mine_half = some(core * half, half)
    gx[x] = gs[mine_half, :] + gcore[mine_half, :]
    for k in (2, 1, 3):
        start(gx.at[x], gx.at[x], send.at[12], recv.at[12], at_x(k)[1])
    sent.append((gx.at[0 : NX - 1], 12))
    mix(2)

    wait(ztx, recv.at[13])
    total = zh[some(x * part, part), :]
    for k in range(NX - 1):
        total = total + ztx[k]
    zx[...] = total
    start(zx, ztz, send.at[14], recv.at[14], other_rep)
    sent.append((zx, 14))

    wait(gx.at[0 : NX - 1], recv.at[12])
    gall[mine_half, :] = gx[0] + gx[1] + gx[2] + gx[3]
    own_g = gall.at[mine_half, :]
    start(own_g, own_g, send.at[11], recv.at[11], other_core)
    sent.append((own_g, 11))
    mix(3)

    wait(zbuf, recv.at[8])
    block_v = vg.at[some(y * yrows, yrows), :]
    for k in (2, 1, 3):
        start(block_v, block_v, send.at[17], recv.at[17], at_y(k)[1])
    sent.append((ybuf, 17))

    wait(own_g, recv.at[11])
    inverse_cholesky(gall[...], inv_ref, 4)
    inverse = inv_ref[...]
    mix(4)

    wait(ztz, recv.at[14])
    own_z = zta.at[pl.ds(pl.multiple_of(core * half + x * part, part), part), :]
    own_z[...] = zx[...] + ztz[...]
    for k in (2, 1, 3):
        start(own_z, own_z, send.at[15], recv.at[15], at_x(k)[1])
    sent.append((ztx, 15))
    mix(5)
    mix(6)

    wait(ybuf, recv.at[17])
    small16 = small.astype(BF16)
    t = [dot(small16, vg[a * SMALL : (a + 1) * SMALL, :]) for a in range(NX)]
    for a, v in enumerate(four(t)):
        basis_ref[a * SMALL : (a + 1) * SMALL, :] = lax.dot_general(
            v * scale, inverse, (((1,), (1,)), ((), ())), precision=HIGH, preferred_element_type=F32
        )

    wait(ztx, recv.at[15])
    half_z = zta.at[mine_half, :]
    start(half_z, half_z, send.at[16], recv.at[16], other_core)
    sent.append((ztc, 16))
    wait(ztc, recv.at[16])
    right = dot(inverse, zta[...], precision=HIGH) * (1.0 / REPLICAS)
    right16 = right.astype(BF16)
    for g in range(groups):
        qf_ref[lanes(g), :] = right[:, g * LANES : (g + 1) * LANES].T

    for g in range(groups):
        wait(rot.at[g, 0 : NX - 1], bsem.at[g])
        for a in range(NX):
            part_rows = pl.ds(a * SMALL, SMALL)
            approx = dot(basis_ref[part_rows, :].astype(BF16), right16[:, g * LANES : (g + 1) * LANES])
            err_ref[part_rows, lanes(g)] = (rot[g, a].astype(F32) - approx).astype(BF16)
    for ref, s in sent:
        wait(ref, send.at[s])


def local(accumulated, signs, q_start):
    rows, cols = accumulated.shape
    rank = q_start.shape[1]
    quarter, yrows = rows // NX, rows // NY
    zrows, half, part = yrows // NZ, rank // NCORE, rank // NPOS
    groups = cols // LANES
    vmem = pl.BlockSpec(memory_space=pltpu.VMEM)
    anywhere = pl.BlockSpec(memory_space=pl.ANY)
    dma = pltpu.SemaphoreType.DMA
    chunk = (groups, NX, quarter, LANES)
    scratch = [
        ((rows, cols), BF16), ((rows * NPOS // LANES, LANES), jnp.int32), ((cols, rank), BF16),
        ((groups, rows, LANES), BF16), (chunk, BF16), (chunk, BF16), (chunk, BF16), (chunk, BF16),
        ((2 * NX, SMALL, SMALL), BF16),
        ((rows, rank), F32), ((rows, rank), BF16), ((NY - 1, yrows, rank), BF16),
        ((yrows, rank), BF16), ((NZ - 1, zrows, rank), BF16), ((NPOS, zrows, rank), F32),
        ((rows, rank), BF16), ((rows, rank), BF16),
        ((rank, rank), F32), ((rank, rank), F32), ((NX, half, rank), F32), ((rank, rank), F32),
        ((rank, cols), F32), ((half, cols), F32), ((half, cols), F32), ((NX - 1, part, cols), F32),
        ((part, cols), F32), ((part, cols), F32), ((rank, cols), F32), ((rank, rank), F32),
    ]
    return pl.pallas_call(
        kernel,
        out_shape=(
            jax.ShapeDtypeStruct((rows, cols), BF16),
            jax.ShapeDtypeStruct((rows, rank), F32),
            jax.ShapeDtypeStruct((cols, rank), F32),
        ),
        in_specs=[anywhere] * 3,
        out_specs=(vmem,) * 3,
        scratch_shapes=[pltpu.VMEM(shape, kind) for shape, kind in scratch]
        + [dma((18,)), dma((18,)), dma((groups,)), dma((groups,)), dma((groups,)), dma((3,))],
        compiler_params=pltpu.CompilerParams(
            collective_id=0, has_side_effects=True, vmem_limit_bytes=48 * 1024 * 1024
        ),
        name="powersgd",
    )(accumulated, signs.reshape(-1, LANES), q_start)


def solution(mesh):
    in_specs = (P("dp", "mp"), P(), P("mp", None))
    out_specs = (P("dp", "mp"), P("dp", None), P("mp", None))
    return jax.shard_map(local, mesh=mesh, in_specs=in_specs, out_specs=out_specs, check_vma=False)
```
